512 devices in a mesh: patch: 128 (over y, z, core), sub: 4 (over x).
Axes of the slice: x: 4, y: 4, z: 16, core: 2. Of those that a mesh axis runs over, the one named last changes fastest.
Arguments:
- pieces: bfloat16 [128, 4, 512, 2048], P('patch', 'sub'), may hold values from -10 to 10
- piece_slot: int32 [128, 4, 512], P('patch', 'sub'), may hold values from 0 to 1023, as said below
- piece_cell: int32 [128, 4, 512], P('patch', 'sub'), may hold values from 0 to 31
- weights: bfloat16 [128, 4, 512], P('patch', 'sub'), may hold values from 0.25 to 4
- science: bfloat16 [128, 512, 512], P('patch', 'sub'), may hold values from -12.5 to 12.5
- good_stamps: int32 [128, 32, 32], P('patch', 'sub'), may hold values 0 or 1
Outputs:
- difference: bfloat16 [128, 512, 512], P('patch', 'sub')
- coefficients: float32 [128, 19], P('patch')
The draws below stay inside these ranges and needn't reach their ends.
Inputs may be any that keep to these rules, and one draw needn't show every extreme that they name: `piece_slot`: on each device the slots are distinct. Slot s stands for destination patch (s // 2) // 4, band (s // 2) % 4, place s % 2. In every draw one destination band, drawn from the seed, receives 2 pieces from every device.
All inputs are finite; a program needn't handle non-finite values. No bound on the sum of `good_stamps` on one device may be relied on, other than what follows from the above.
Results may differ from the reference program's by a relative error of at most 0.0094.
The reference program's roundings to bfloat16 on the way count: a program that leaves them out, or rounds other values in their place, can miss the bound.
Values may be sent and summed in bfloat16 or wider, within the bound.
A program may use at most 64 MiB of HBM per device.

```python
import math
import jax
import jax.numpy as jnp
import numpy as np
from jax import lax

BAND = 128
WIDTH = 512
PR = 16
PC = 128
STAMP = 16
CAP = 2
KSIZE = 23
DEGREE = 2
HALF = 11
NBASIS = 18
UNKNOWNS = 19
PATCHES = 128
BANDS = 4
ROWS = 512
CELLS = 32
SLOTS = 1024
PIECES_DEV = 512


def route_table(key):
    hot_key, device_key = jax.random.split(key)
    devices = SLOTS // CAP
    hottest = jax.random.randint(hot_key, (), 0, devices, dtype=jnp.int32)

    def one_device(own_key):
        keys = jax.random.split(own_key, 3)
        picked = jax.random.permutation(keys[0], (devices - 1) * CAP)[:PIECES_DEV - CAP].astype(jnp.int32)
        target = picked // CAP
        target = target + (target >= hottest).astype(jnp.int32)
        slots = jnp.concatenate([hottest * CAP + jnp.arange(CAP, dtype=jnp.int32), target * CAP + picked % CAP])
        order = jax.random.permutation(keys[1], PIECES_DEV)
        cells = jax.random.randint(keys[2], (PIECES_DEV,), 0, CELLS, dtype=jnp.int32)
        return (slots[order], cells)
    slots, cells = jax.vmap(one_device)(jax.random.split(device_key, devices))
    return (slots.reshape(PATCHES, BANDS, PIECES_DEV), cells.reshape(PATCHES, BANDS, PIECES_DEV))


def sky_values(key, identity):

    def one_cell(cell_id):
        cell_key = jax.random.fold_in(key, cell_id)
        values = jax.random.normal(cell_key, (PR * PC,), jnp.float32)
        return jnp.clip(values, -5.0, 5.0)
    return jax.vmap(one_cell)(identity)


def noise_values(key, shape):
    values = jax.random.normal(key, shape, jnp.float32)
    return jnp.clip(values, -5.0, 5.0)


def draw_piece_slot(key, part):
    return route_table(jax.random.fold_in(key, 101))[0]


def draw_piece_cell(key, part):
    return route_table(jax.random.fold_in(key, 101))[1]


def draw_pieces(key, part):
    slots, cells = route_table(jax.random.fold_in(key, 101))
    devices = PATCHES * BANDS
    identity = (slots // CAP * CELLS + cells).reshape(devices, PIECES_DEV)
    sky_key = jax.random.fold_in(key, 202)
    noise_key = jax.random.fold_in(key, 303)

    def one_device(inputs):
        number, cell_ids = inputs
        sky = sky_values(sky_key, cell_ids)
        noise = noise_values(jax.random.fold_in(noise_key, number), (PIECES_DEV, PR * PC))
        return (sky + noise).astype(jnp.bfloat16)
    result = lax.map(one_device, (jnp.arange(devices, dtype=jnp.int32), identity))
    return result.reshape(PATCHES, BANDS, PIECES_DEV, PR * PC)


def draw_science(key, part):
    devices = PATCHES * BANDS
    sky_key = jax.random.fold_in(key, 202)
    identity = jnp.arange(devices * CELLS, dtype=jnp.int32).reshape(devices, CELLS)
    sky = lax.map(lambda cell_ids: sky_values(sky_key, cell_ids), identity)
    sky = sky.reshape(PATCHES, BANDS, BAND // PR, WIDTH // PC, PR, PC)
    sky = sky.transpose(0, 1, 2, 4, 3, 5).reshape(PATCHES, ROWS, WIDTH)
    beside = jnp.concatenate([sky[:, :, 1:], jnp.zeros((PATCHES, ROWS, 1), jnp.float32)], axis=2)
    spread = 1.2 * (jnp.arange(ROWS, dtype=jnp.float32) + 0.5) / ROWS
    noise = noise_values(jax.random.fold_in(key, 404), (PATCHES, ROWS, WIDTH))
    return (sky + spread[None, :, None] * beside + 0.3 * noise).astype(jnp.bfloat16)


def touch_ends(values, stream_key, low, high):
    longest = values.shape.index(max(values.shape))
    spots = []
    for shift in (0, 1):
        where = [jax.random.randint(jax.random.fold_in(stream_key, axis), (), 0, length) for axis, length in enumerate(values.shape)]
        where[longest] = (where[longest] + shift) % values.shape[longest]
        spots.append(tuple(where))
    return values.at[spots[0]].set(low).at[spots[1]].set(high)


def levels(rng, shape, cuts, smallest, top_value):
    level, own = 1.0, jax.random.fold_in(rng, 6)
    for axis_at, shards_of in cuts:
        draws = jnp.exp(jax.random.uniform(jax.random.fold_in(own, axis_at), (shards_of,), jnp.float32, smallest / len(cuts), top_value / len(cuts)))
        level = level * jnp.repeat(draws, shape[axis_at] // shards_of).reshape([-1 if axis == axis_at else 1 for axis in range(len(shape))])
    return level


def setup_inputs(seed: int = 0) -> dict:
    key_list = jax.random.split(jax.random.key(seed), 7)
    return {
        "pieces": draw_pieces(jax.random.fold_in(key_list[6], 71), 0),
        "piece_slot": draw_piece_slot(jax.random.fold_in(key_list[6], 71), 0),
        "piece_cell": draw_piece_cell(jax.random.fold_in(key_list[6], 71), 0),
        "weights": jnp.clip(jnp.exp(math.log(4.0) - 2.7725887 * jax.random.uniform(key_list[3], (PATCHES, BANDS, PIECES_DEV), jnp.float32) ** levels(key_list[3], (PATCHES, BANDS, PIECES_DEV), ((0, 128), (1, 4)), -0.2, 0.2)), 0.25, 4.0).astype(jnp.bfloat16),
        "science": draw_science(jax.random.fold_in(key_list[6], 71), 0),
        "good_stamps": touch_ends((jax.random.randint(key_list[5], (PATCHES, ROWS // STAMP, WIDTH // STAMP), 0, 8) < 7).astype(jnp.int32), jax.random.fold_in(key_list[5], 1), 0, 1),
    }


SIGMAS = (0.75, 1.5, 3.0)
RIDGE = 0.1
BASIS_PAIRS = ((0, 0), (1, 0), (0, 1), (2, 0), (1, 1), (0, 2))

def filter_table():
    result = []
    for sigma in SIGMAS:
        for power in range(DEGREE + 1):
            entries = []
            for offset in range(KSIZE):
                position = float(offset - HALF)
                entries.append(math.exp(-position * position / (2.0 * sigma * sigma)) * (position / sigma) ** power)
            norm_value = math.sqrt(sum([entry * entry for entry in entries]))
            result.append([entry / norm_value for entry in entries])
    return np.array(result, dtype=np.float32)

def basis_terms():
    return [(gauss, pair[0], pair[1]) for gauss in range(len(SIGMAS)) for pair in BASIS_PAIRS]

def fit_patch(inputs):
    template, science_img, good = inputs
    filters = jnp.asarray(filter_table()).astype(jnp.bfloat16).astype(jnp.float32)
    padded = jnp.pad(template.astype(jnp.float32), ((HALF, HALF), (0, 0)))
    shifted = jnp.stack([padded[shift:shift + ROWS] for shift in range(KSIZE)])
    vertical = jnp.einsum('fs,srw->frw', filters, shifted).astype(jnp.bfloat16)
    images = {}
    for gauss in range(len(SIGMAS)):
        for power_v in range(DEGREE + 1):
            source = jnp.pad(vertical[gauss * (DEGREE + 1) + power_v].astype(jnp.float32), ((0, 0), (HALF, HALF)))
            columns = jnp.stack([source[:, shift:shift + WIDTH] for shift in range(KSIZE)])
            count = DEGREE + 1 - power_v
            first = gauss * (DEGREE + 1)
            result = jnp.einsum('is,srw->irw', filters[first:first + count], columns).astype(jnp.bfloat16)
            for power_h in range(count):
                images[gauss, power_h, power_v] = result[power_h]
    basis = jnp.stack([images[term] for term in basis_terms()])
    mask = jnp.repeat(jnp.repeat(good, STAMP, axis=0), STAMP, axis=1) == 1
    design = jnp.concatenate([basis, jnp.ones((1, ROWS, WIDTH), jnp.bfloat16), science_img[None]], axis=0)
    design = design.reshape(NBASIS + 2, ROWS * WIDTH)
    masked = jnp.where(mask.reshape(1, ROWS * WIDTH), design, jnp.zeros((), jnp.bfloat16))
    gram = jnp.dot(masked.astype(jnp.float32), design.T.astype(jnp.float32), preferred_element_type=jnp.float32)
    normal = gram[:UNKNOWNS, :UNKNOWNS]
    rhs = gram[:UNKNOWNS, UNKNOWNS]
    normal = normal + RIDGE * jnp.diag(jnp.diag(normal))
    factor = jnp.linalg.cholesky(normal)
    middle = lax.linalg.triangular_solve(factor, rhs[:, None], left_side=True, lower=True)
    solution = lax.linalg.triangular_solve(factor, middle, left_side=True, lower=True, transpose_a=True)[:, 0]
    model = jnp.zeros((ROWS, WIDTH), jnp.float32) + solution[NBASIS]
    for index in range(NBASIS):
        model = model + solution[index] * basis[index].astype(jnp.float32)
    difference = jnp.where(mask, science_img.astype(jnp.float32) - model, jnp.float32(0.0))
    return (difference.astype(jnp.bfloat16), solution)

def reference(pieces, piece_slot, piece_cell, weights, science, good_stamps):
    devices = PATCHES * BANDS
    features = PR * PC
    all_pieces = pieces.reshape(devices, PIECES_DEV, features)
    all_slots = piece_slot.reshape(devices, PIECES_DEV)
    all_cells = piece_cell.reshape(devices, PIECES_DEV)
    all_weights = weights.reshape(devices, PIECES_DEV)

    def add_source(carry, inputs):
        numer, wsum = carry
        block, slots, cells, weight = inputs
        target = (slots // CAP * CELLS + cells).astype(jnp.int32)
        numer = numer.at[target].add(weight.astype(jnp.float32)[:, None] * block.astype(jnp.float32))
        wsum = wsum.at[target].add(weight.astype(jnp.float32))
        return ((numer, wsum), None)
    start = (jnp.zeros((devices * CELLS, features), jnp.float32), jnp.zeros((devices * CELLS,), jnp.float32))
    (numer, wsum), _ = lax.scan(add_source, start, (all_pieces, all_slots, all_cells, all_weights))
    template = (numer / jnp.maximum(wsum, 1.0)[:, None]).astype(jnp.bfloat16)
    template = template.reshape(PATCHES, BANDS, BAND // PR, WIDTH // PC, PR, PC)
    template = template.transpose(0, 1, 2, 4, 3, 5).reshape(PATCHES, ROWS, WIDTH)
    difference, coefficients = lax.map(fit_patch, (template, science, good_stamps))
    return (difference, coefficients)
```

```python
import functools
import math

import jax
import jax.numpy as jnp
import numpy as np
from jax import lax
from jax.experimental import pallas as pl
from jax.experimental.pallas import tpu as pltpu
from jax.sharding import PartitionSpec as P

MESH = pl.DeviceIdType.MESH
F32 = jnp.float32
BF16 = jnp.bfloat16

NX, NY, NZ, NC = 4, 4, 16, 2
PEERS = NX * NY * NC
ROWS = 16
BAND = 128
WIDTH = 512
KSIZE = 23
DEGREE = 2
HALF = 11
SIGMAS = (0.75, 1.5, 3.0)
RIDGE = 0.1
BASIS_PAIRS = ((0, 0), (1, 0), (0, 1), (2, 0), (1, 1), (0, 2))
FEAT = 1024
TAIL = 128


def filter_table():
    result = []
    for sigma in SIGMAS:
        for power in range(DEGREE + 1):
            entries = []
            for offset in range(KSIZE):
                position = float(offset - HALF)
                entries.append(
                    math.exp(-position * position / (2.0 * sigma * sigma))
                    * (position / sigma) ** power
                )
            norm_value = math.sqrt(sum([entry * entry for entry in entries]))
            result.append([entry / norm_value for entry in entries])
    return np.array(result, dtype=np.float32)


def vertical_matrix():
    filters = filter_table()
    matrix = np.zeros((9, BAND, 256), np.float32)
    for row in range(BAND):
        for v in range(-HALF, HALF + 1):
            source = row + v
            if source < 0:
                column = BAND + ROWS + source
            elif source >= BAND:
                column = BAND + ROWS + source - BAND
            else:
                column = source
            matrix[:, row, column] = filters[:, v + HALF]
    return matrix.reshape(9 * BAND, 256).astype(jnp.bfloat16)


def horizontal_matrix():
    filters = filter_table()
    matrix = np.zeros((9, WIDTH, WIDTH), np.float32)
    for u in range(-HALF, HALF + 1):
        x = np.arange(max(0, -u), min(WIDTH, WIDTH - u))
        matrix[:, x + u, x] = filters[:, u + HALF][:, None]
    return matrix.astype(jnp.bfloat16)


def iota(shape, axis):
    return lax.broadcasted_iota(jnp.int32, shape, axis)


def kernel(
    slot_ref, cell_ref, weight_ref, science_ref, good_ref, pieces_hbm, vert_hbm, horiz_hbm,
    diff_ref, coef_ref,
    pieces, vert, horiz, onehot, send0, send1, recv0, recv1, place,
    part0, part1, ring0, ring1, tmpl, window, halo, vimg, design, gram_mine, gram_all,
    local_sem, a2a_send, a2a_recv, ring_send, ring_recv, halo_send, halo_recv, gram_send, gram_recv,
):
    p = lax.axis_index("patch")
    x = lax.axis_index("sub")
    c = lax.rem(p, NC)
    z = lax.rem(lax.div(p, NC), NZ)
    y = lax.div(p, NC * NZ)

    def patch_of(yy, zz, cc):
        return (yy * NZ + zz) * NC + cc

    load_pieces = pltpu.make_async_copy(pieces_hbm.at[0, 0], pieces, local_sem.at[0])
    load_vert = pltpu.make_async_copy(vert_hbm, vert, local_sem.at[1])
    load_horiz = pltpu.make_async_copy(horiz_hbm, horiz, local_sem.at[2])
    load_pieces.start()

    barrier = pltpu.get_barrier_semaphore()

    def peer(r):
        dy = lax.div(r, NC * NX)
        dc = lax.rem(lax.div(r, NX), NC)
        dx = lax.rem(r, NX)
        return (
            patch_of(lax.rem(y + dy, NY), z, lax.rem(c + dc, NC)),
            lax.rem(x + dx, NX),
        )

    up = (patch_of(y, lax.rem(z + 1, NZ), c), x)
    down = (patch_of(y, lax.rem(z + NZ - 1, NZ), c), x)

    def greet(r, carry):
        pl.semaphore_signal(barrier, inc=1, device_id=peer(r), device_id_type=MESH)
        return carry

    lax.fori_loop(1, PEERS, greet, 0)
    pl.semaphore_signal(barrier, inc=1, device_id=up, device_id_type=MESH)
    pl.semaphore_signal(barrier, inc=1, device_id=down, device_id_type=MESH)

    slots = slot_ref[0]
    cells = cell_ref[0]
    weights = weight_ref[0].astype(F32)
    marks = (lax.rem(cells, 4) * 8 + lax.div(cells, 4)).astype(F32)
    row = iota((128, 1), 0)
    peer_in = lax.div(row, ROWS)
    cc = lax.rem(c + lax.div(peer_in, NX), NC)
    xx = lax.rem(x + lax.rem(peer_in, NX), NX)
    within = lax.rem(row, ROWS)
    base = []
    for g in range(2):
        j = lax.div(within, 2) + 8 * g
        half = lax.div(j + 1, 2)
        off = jnp.where(lax.rem(j, 2) == 1, 8 - half, half - 8)
        zz = lax.rem(z + off + NZ, NZ)
        base.append(zz * 16 + cc * 8 + xx * 2 + lax.rem(within, 2))
    lane = iota((128, TAIL), 1)

    def select(dy, carry):
        yy = lax.rem(y + dy, NY)
        shifted = slots - yy * 256
        tail = jnp.zeros((128, TAIL), F32)
        for g in range(2):
            hit = shifted == base[g]
            onehot[g, dy] = jnp.where(hit, 1.0, 0.0).astype(BF16)
            w = jnp.sum(jnp.where(hit, weights, 0.0), axis=1, keepdims=True)
            m = jnp.sum(jnp.where(hit, marks, 0.0), axis=1, keepdims=True)
            tail = jnp.where(lane == 2 * g, w, jnp.where(lane == 2 * g + 1, m, tail))
        send0[pl.ds(dy * 8, 8), :, FEAT:] = tail.astype(BF16).reshape(8, ROWS, TAIL)
        return carry

    lax.fori_loop(0, NY, select, 0)
    recv0[0, :, FEAT:] = send0[0, :, FEAT:]

    load_pieces.wait()
    load_vert.start()
    load_horiz.start()

    def pack(chunk):
        g, h = chunk // 2, chunk % 2

        def body(dy, carry):
            picked = jnp.dot(
                onehot[g, dy], pieces[:, h * FEAT : (h + 1) * FEAT], preferred_element_type=F32
            )
            picked = picked.astype(BF16).reshape(8, ROWS, FEAT)
            if chunk == 0:
                send0[pl.ds(dy * 8, 8), :, :FEAT] = picked

                @pl.when(dy == 0)
                def _():
                    recv0[0, :, :FEAT] = picked[0]
            else:
                send1[chunk - 1, pl.ds(dy * 8, 8)] = picked

                @pl.when(dy == 0)
                def _():
                    recv1[chunk - 1, 0] = picked[0]
            return carry

        lax.fori_loop(0, NY, body, 0)

    def ends(chunk):
        if chunk == 0:
            return send0, recv0
        return send1.at[chunk - 1], recv1.at[chunk - 1]

    def send(chunk):
        source, target = ends(chunk)

        def body(r, carry):
            pltpu.make_async_remote_copy(
                src_ref=source.at[r],
                dst_ref=target.at[r],
                send_sem=a2a_send.at[chunk],
                recv_sem=a2a_recv.at[chunk],
                device_id=peer(r),
                device_id_type=MESH,
            ).start()
            return carry

        lax.fori_loop(1, PEERS, body, 0)

    def arrived(chunk):
        _, target = ends(chunk)
        rest = target.at[pl.ds(1, PEERS - 1)]
        pltpu.make_async_copy(rest, rest, a2a_recv.at[chunk]).wait()

    def sent(chunk):
        source, _ = ends(chunk)
        rest = source.at[pl.ds(1, PEERS - 1)]
        pltpu.make_async_copy(rest, rest, a2a_send.at[chunk]).wait()

    def placing(g):
        labels = recv0[:, :, FEAT:].reshape(PEERS * ROWS, TAIL).astype(F32)
        w = labels[:, 2 * g : 2 * g + 1]
        m = labels[:, 2 * g + 1 : 2 * g + 2]
        plane = lax.div(lax.rem(iota((PEERS * ROWS, 1), 0), ROWS), 2)
        key = m + (plane * 32).astype(F32)
        at = iota((PEERS * ROWS, 256), 1).astype(F32)
        spread = jnp.where(at == key, w, 0.0).T
        place[g] = spread.astype(BF16)
        total = jnp.sum(spread, axis=1, keepdims=True)
        part0[8 * g : 8 * g + 8, :, FEAT:] = jnp.broadcast_to(total, (256, TAIL)).reshape(8, 32, TAIL)

    def accumulate(chunk):
        g, h = chunk // 2, chunk % 2
        _, got = ends(chunk)
        into = part0 if h == 0 else part1
        for t in range(FEAT // 256):
            block = got[:, :, t * 256 : (t + 1) * 256].reshape(PEERS * ROWS, 256)
            numer = jnp.dot(place[g], block, preferred_element_type=F32)
            into[8 * g : 8 * g + 8, :, t * 256 : (t + 1) * 256] = numer.reshape(8, 32, 256)

    parts, rings = (part0, part1), (ring0, ring1)

    def hop(h, way, k):
        index = 0 if k == 0 else (2 * k - 1 if way == 0 else 2 * k)
        return pltpu.make_async_remote_copy(
            src_ref=parts[h].at[index],
            dst_ref=rings[h].at[way, k],
            send_sem=ring_send.at[h, way, k],
            recv_sem=ring_recv.at[h, way, k],
            device_id=up if way == 0 else down,
            device_id_type=MESH,
        )

    def step(h, k):
        for way in range(2):
            if k == 0:
                if way == h:
                    hop(h, way, 0).start()
                continue
            if k > 1 or way == h:
                hop(h, way, k - 1).wait_recv()
                index = 2 * k - 1 if way == 0 else 2 * k
                parts[h][index] += rings[h][way, k - 1]
            hop(h, way, k).start()

    def finish(h):
        for way in range(2):
            hop(h, way, 7).wait_recv()
        parts[h][15] += rings[h][0, 7] + rings[h][1, 7]

    pl.semaphore_wait(barrier, PEERS + 1)
    pack(0)
    send(0)
    pack(1)
    send(1)
    pack(2)
    pack(3)
    arrived(0)
    send(2)
    placing(0)
    accumulate(0)
    step(0, 0)
    step(0, 1)
    placing(1)
    arrived(1)
    send(3)
    accumulate(1)
    step(1, 0)
    step(0, 2)
    step(1, 1)
    step(0, 3)
    step(1, 2)
    arrived(2)
    accumulate(2)
    step(0, 4)
    step(1, 3)
    step(0, 5)
    arrived(3)
    accumulate(3)
    step(1, 4)
    step(0, 6)
    step(1, 5)
    step(0, 7)
    step(1, 6)
    step(1, 7)
    finish(0)

    weight_sum = jnp.maximum(part0[15, :, FEAT:], 1.0)
    for r in range(8):
        t = part0[15, :, r * 128 : (r + 1) * 128] / weight_sum
        for b in range(4):
            tmpl[b, pl.ds(r, 8, stride=16), :] = t[8 * b : 8 * b + 8]
    finish(1)
    for r in range(8):
        t = part1[15, :, r * 128 : (r + 1) * 128] / weight_sum
        for b in range(4):
            tmpl[b, pl.ds(r + 8, 8, stride=16), :] = t[8 * b : 8 * b + 8]
    for b in range(4):
        window[0:BAND, 128 * b : 128 * (b + 1)] = tmpl[b].astype(BF16)

    below = pltpu.make_async_remote_copy(
        src_ref=window.at[pl.ds(BAND - ROWS, ROWS)], dst_ref=halo.at[0],
        send_sem=halo_send.at[0], recv_sem=halo_recv.at[0],
        device_id=(p, lax.rem(x + 1, NX)), device_id_type=MESH,
    )
    above = pltpu.make_async_remote_copy(
        src_ref=window.at[pl.ds(0, ROWS)], dst_ref=halo.at[1],
        send_sem=halo_send.at[1], recv_sem=halo_recv.at[1],
        device_id=(p, lax.rem(x + NX - 1, NX)), device_id_type=MESH,
    )
    below.start()
    above.start()

    stamp_rows = jnp.where(lax.div(iota((BAND, 8), 0), 16) == iota((BAND, 8), 1), 1.0, 0.0)
    stamp_cols = jnp.where(lax.div(iota((32, WIDTH), 1), 16) == iota((32, WIDTH), 0), 1.0, 0.0)
    good = jnp.where(good_ref[0] == 1, 1.0, 0.0)
    mask = jnp.dot(jnp.dot(stamp_rows, good, preferred_element_type=F32), stamp_cols, preferred_element_type=F32)
    design[:, 18] = mask.astype(BF16).reshape(8, ROWS, WIDTH)
    design[:, 19] = (science_ref[0].astype(F32) * mask).astype(BF16).reshape(8, ROWS, WIDTH)
    window[BAND + 2 * ROWS :, :] = jnp.zeros((256 - BAND - 2 * ROWS, WIDTH), BF16)
    load_vert.wait()
    load_horiz.wait()

    below.wait_recv()
    above.wait_recv()
    window[BAND : BAND + ROWS, :] = jnp.where(x > 0, halo[0].astype(F32), 0.0).astype(BF16)
    window[BAND + ROWS : BAND + 2 * ROWS, :] = jnp.where(x < NX - 1, halo[1].astype(F32), 0.0).astype(BF16)

    for f in range(3):
        rows = slice(f * 3 * BAND, (f + 1) * 3 * BAND)
        vimg[rows] = jnp.dot(vert[rows], window[...], preferred_element_type=F32).astype(BF16)

    for g in range(3):
        for i in range(3):
            count = (3 - i) * BAND
            image = jnp.dot(
                vimg[g * 3 * BAND : g * 3 * BAND + count], horiz[g * 3 + i], preferred_element_type=F32
            )
            for j in range(3 - i):
                k = g * 6 + BASIS_PAIRS.index((i, j))
                part = image[j * BAND : (j + 1) * BAND].astype(BF16).astype(F32) * mask
                design[:, k] = part.astype(BF16).reshape(8, ROWS, WIDTH)

    def product(q, total):
        block = design[q].reshape(20 * ROWS, WIDTH)
        return total + lax.dot_general(
            block, block, (((1,), (1,)), ((), ())), preferred_element_type=F32
        )

    total = lax.fori_loop(0, 8, product, jnp.zeros((20 * ROWS, 20 * ROWS), F32))
    same = lax.rem(iota((320, 320), 0), ROWS) == lax.rem(iota((320, 320), 1), ROWS)
    total = jnp.sum(jnp.where(same, total, 0.0).reshape(20, ROWS, 320), axis=1)
    fold = jnp.where(lax.div(iota((320, 128), 0), ROWS) == iota((320, 128), 1), 1.0, 0.0)
    normal = jnp.dot(total, fold, preferred_element_type=F32, precision=lax.Precision.HIGHEST)
    normal = jnp.concatenate([normal, jnp.zeros((4, 128), F32)], axis=0)
    gram_mine[...] = normal
    gram_all[x] = normal

    shares = [
        pltpu.make_async_remote_copy(
            src_ref=gram_mine, dst_ref=gram_all.at[x],
            send_sem=gram_send.at[d - 1], recv_sem=gram_recv.at[d - 1],
            device_id=(p, lax.rem(x + d, NX)), device_id_type=MESH,
        )
        for d in range(1, NX)
    ]
    for share in shares:
        share.start()
    for share in shares:
        share.wait_recv()
    normal = gram_all[0] + gram_all[1] + gram_all[2] + gram_all[3]

    rows = iota((24, 128), 0)
    lanes = iota((24, 128), 1)
    diagonal = (rows == lanes) & (rows < 19)
    system = normal + jnp.where(diagonal, RIDGE * normal, 0.0)
    for k in range(19):
        pivot_row = system[k : k + 1] / system[k : k + 1, k : k + 1]
        column = jnp.where(rows[:, :1] == k, 0.0, system[:, k : k + 1])
        system = system - column * pivot_row
    rhs = system[:, 19:20]
    lead = jnp.sum(jnp.where(diagonal, system, 0.0), axis=1, keepdims=True)
    solved = rhs / jnp.where(rows[:, :1] < 19, lead, 1.0)
    coef_ref[...] = jnp.sum(jnp.where(diagonal, solved, 0.0), axis=0, keepdims=True)[:, :19]

    def model(q, carry):
        value = design[q, 19].astype(F32)
        for k in range(19):
            value = value - solved[k : k + 1] * design[q, k].astype(F32)
        diff_ref[0, pl.ds(q * ROWS, ROWS), :] = value.astype(BF16)
        return carry

    lax.fori_loop(0, 8, model, 0)

    for chunk in range(4):
        sent(chunk)
    for h in range(2):
        for way in range(2):
            for k in range(8):
                if k > 0 or way == h:
                    hop(h, way, k).wait_send()
    below.wait_send()
    above.wait_send()
    for share in shares:
        share.wait_send()


def shards(pieces, piece_slot, piece_cell, weights, science, good_stamps):
    vmem = pl.BlockSpec(memory_space=pltpu.VMEM)
    anywhere = pl.BlockSpec(memory_space=pl.ANY)
    dma = pltpu.SemaphoreType.DMA
    return pl.pallas_call(
        kernel,
        out_shape=(
            jax.ShapeDtypeStruct((1, BAND, WIDTH), BF16),
            jax.ShapeDtypeStruct((1, 19), F32),
        ),
        in_specs=[vmem] * 5 + [anywhere] * 3,
        out_specs=(vmem, vmem),
        scratch_shapes=[
            pltpu.VMEM((512, 2048), BF16),
            pltpu.VMEM((9 * BAND, 256), BF16),
            pltpu.VMEM((9, WIDTH, WIDTH), BF16),
            pltpu.VMEM((2, NY, 128, 512), BF16),
            pltpu.VMEM((PEERS, ROWS, FEAT + TAIL), BF16),
            pltpu.VMEM((3, PEERS, ROWS, FEAT), BF16),
            pltpu.VMEM((PEERS, ROWS, FEAT + TAIL), BF16),
            pltpu.VMEM((3, PEERS, ROWS, FEAT), BF16),
            pltpu.VMEM((2, 256, PEERS * ROWS), BF16),
            pltpu.VMEM((NZ, 32, FEAT + TAIL), F32),
            pltpu.VMEM((NZ, 32, FEAT), F32),
            pltpu.VMEM((2, 8, 32, FEAT + TAIL), F32),
            pltpu.VMEM((2, 8, 32, FEAT), F32),
            pltpu.VMEM((4, BAND, 128), F32),
            pltpu.VMEM((256, WIDTH), BF16),
            pltpu.VMEM((2, ROWS, WIDTH), BF16),
            pltpu.VMEM((9 * BAND, WIDTH), BF16),
            pltpu.VMEM((8, 20, ROWS, WIDTH), BF16),
            pltpu.VMEM((24, 128), F32),
            pltpu.VMEM((NX, 24, 128), F32),
            dma((3,)),
            dma((4,)),
            dma((4,)),
            dma((2, 2, 8)),
            dma((2, 2, 8)),
            dma((2,)),
            dma((2,)),
            dma((3,)),
            dma((3,)),
        ],
        compiler_params=pltpu.CompilerParams(
            collective_id=0, has_side_effects=True, vmem_limit_bytes=56 * 2**20
        ),
    )(
        piece_slot[0], piece_cell[0], weights[0], science, good_stamps, pieces,
        jnp.asarray(vertical_matrix()), jnp.asarray(horizontal_matrix()),
    )


def solution(mesh):
    in_specs = (
        P("patch", "sub", None, None),
        P("patch", "sub", None),
        P("patch", "sub", None),
        P("patch", "sub", None),
        P("patch", "sub", None),
        P("patch", "sub", None),
    )
    out_specs = (P("patch", "sub", None), P("patch", None))
    return jax.shard_map(shards, mesh=mesh, in_specs=in_specs, out_specs=out_specs, check_vma=False)
```

```python
import functools
import math

import jax
import jax.numpy as jnp
import numpy as np
from jax import lax
from jax.experimental import pallas as pl
from jax.experimental.pallas import tpu as pltpu
from jax.sharding import PartitionSpec as P

MESH = pl.DeviceIdType.MESH
F32 = jnp.float32
BF16 = jnp.bfloat16

NX, NY, NZ, NC = 4, 4, 16, 2
PEERS = NX * NY * NC
ROWS = 16
BAND = 128
WIDTH = 512
KSIZE = 23
DEGREE = 2
HALF = 11
SIGMAS = (0.75, 1.5, 3.0)
RIDGE = 0.1
BASIS_PAIRS = ((0, 0), (1, 0), (0, 1), (2, 0), (1, 1), (0, 2))
FEAT = 1024
TAIL = 128
LIMIT = 10.0
LEVELS = 32700.0


def filter_table():
    result = []
    for sigma in SIGMAS:
        for power in range(DEGREE + 1):
            entries = []
            for offset in range(KSIZE):
                position = float(offset - HALF)
                entries.append(
                    math.exp(-position * position / (2.0 * sigma * sigma))
                    * (position / sigma) ** power
                )
            norm_value = math.sqrt(sum([entry * entry for entry in entries]))
            result.append([entry / norm_value for entry in entries])
    return np.array(result, dtype=np.float32)


def vertical_matrix():
    filters = filter_table()
    matrix = np.zeros((9, BAND, 256), np.float32)
    for row in range(BAND):
        for v in range(-HALF, HALF + 1):
            source = row + v
            if source < 0:
                column = BAND + ROWS + source
            elif source >= BAND:
                column = BAND + ROWS + source - BAND
            else:
                column = source
            matrix[:, row, column] = filters[:, v + HALF]
    return matrix.reshape(9 * BAND, 256).astype(jnp.bfloat16)


def horizontal_matrix():
    filters = filter_table()
    matrix = np.zeros((9, WIDTH, WIDTH), np.float32)
    for u in range(-HALF, HALF + 1):
        x = np.arange(max(0, -u), min(WIDTH, WIDTH - u))
        matrix[:, x + u, x] = filters[:, u + HALF][:, None]
    return matrix.astype(jnp.bfloat16)


def iota(shape, axis):
    return lax.broadcasted_iota(jnp.int32, shape, axis)


def kernel(
    slot_ref, cell_ref, weight_ref, science_ref, good_ref, pieces_hbm, vert_hbm, horiz_hbm,
    diff_ref, coef_ref,
    pieces, vert, horiz, onehot, send0, send1, recv0, recv1, place,
    part0, part1, out0, out1, ring0, ring1, got, tmpl, window, halo, vimg, design, gram_mine, gram_all,
    local_sem, a2a_send, a2a_recv, ring_send, ring_recv, halo_send, halo_recv, gram_send, gram_recv,
):
    p = lax.axis_index("patch")
    x = lax.axis_index("sub")
    c = lax.rem(p, NC)
    z = lax.rem(lax.div(p, NC), NZ)
    y = lax.div(p, NC * NZ)

    def patch_of(yy, zz, cc):
        return (yy * NZ + zz) * NC + cc

    load_pieces = pltpu.make_async_copy(pieces_hbm.at[0, 0], pieces, local_sem.at[0])
    load_vert = pltpu.make_async_copy(vert_hbm, vert, local_sem.at[1])
    load_horiz = pltpu.make_async_copy(horiz_hbm, horiz, local_sem.at[2])
    load_pieces.start()

    barrier = pltpu.get_barrier_semaphore()

    def peer(r):
        dy = lax.div(r, NC * NX)
        dc = lax.rem(lax.div(r, NX), NC)
        dx = lax.rem(r, NX)
        return (
            patch_of(lax.rem(y + dy, NY), z, lax.rem(c + dc, NC)),
            lax.rem(x + dx, NX),
        )

    up = (patch_of(y, lax.rem(z + 1, NZ), c), x)
    down = (patch_of(y, lax.rem(z + NZ - 1, NZ), c), x)

    def greet(r, carry):
        pl.semaphore_signal(barrier, inc=1, device_id=peer(r), device_id_type=MESH)
        return carry

    lax.fori_loop(1, PEERS, greet, 0)
    pl.semaphore_signal(barrier, inc=1, device_id=up, device_id_type=MESH)
    pl.semaphore_signal(barrier, inc=1, device_id=down, device_id_type=MESH)

    slots = slot_ref[0]
    cells = cell_ref[0]
    weights = weight_ref[0].astype(F32)
    marks = (lax.rem(cells, 4) * 8 + lax.div(cells, 4)).astype(F32)
    row = iota((128, 1), 0)
    peer_in = lax.rem(lax.div(row, 8), NC * NX)
    cc = lax.rem(c + lax.div(peer_in, NX), NC)
    xx = lax.rem(x + lax.rem(peer_in, NX), NX)
    within = lax.rem(row, 8)
    base = []
    for chunk in range(4):
        j = lax.div(within, 2) + 4 * chunk
        half = lax.div(j + 1, 2)
        off = jnp.where(lax.rem(j, 2) == 1, 8 - half, half - 8)
        zz = lax.rem(z + off + NZ, NZ)
        base.append(zz * 16 + cc * 8 + xx * 2 + lax.rem(within, 2))
    lane = iota((128, TAIL), 1)

    def both(a, b, width):
        pair = [t.reshape(16, 8, width) for t in (a, b)]
        return jnp.concatenate(pair, axis=1).astype(BF16)

    def select(two, carry):
        yy = lax.rem(y + 2 * two + lax.div(row, 64), NY) * 256
        tail = jnp.zeros((128, TAIL), F32)
        for chunk in range(4):
            hit = slots == base[chunk] + yy
            onehot[chunk, two] = jnp.where(hit, 1.0, 0.0).astype(BF16)
            w = jnp.sum(jnp.where(hit, weights, 0.0), axis=1, keepdims=True)
            m = jnp.sum(jnp.where(hit, marks, 0.0), axis=1, keepdims=True)
            tail = jnp.where(lane == 2 * chunk, w, jnp.where(lane == 2 * chunk + 1, m, tail))
        send0[pl.ds(two * 16, 16), :, FEAT:] = both(tail, tail, TAIL)
        return carry

    lax.fori_loop(0, 2, select, 0)
    recv0[0, :, FEAT:] = send0[0, :, FEAT:]

    load_pieces.wait()
    load_vert.start()
    load_horiz.start()

    def pack(chunk):
        def body(two, carry):
            a, b = (
                jnp.dot(
                    onehot[chunk, two], pieces[:, h * FEAT : (h + 1) * FEAT], preferred_element_type=F32
                )
                for h in range(2)
            )
            picked = both(a, b, FEAT)
            if chunk == 0:
                send0[pl.ds(two * 16, 16), :, :FEAT] = picked

                @pl.when(two == 0)
                def _():
                    recv0[0, :, :FEAT] = picked[0]
            else:
                send1[chunk - 1, pl.ds(two * 16, 16)] = picked

                @pl.when(two == 0)
                def _():
                    recv1[chunk - 1, 0] = picked[0]
            return carry

        lax.fori_loop(0, 2, body, 0)

    def ends(chunk):
        if chunk == 0:
            return send0, recv0
        return send1.at[chunk - 1], recv1.at[chunk - 1]

    def send(chunk):
        source, target = ends(chunk)

        def body(r, carry):
            pltpu.make_async_remote_copy(
                src_ref=source.at[r],
                dst_ref=target.at[r],
                send_sem=a2a_send.at[chunk],
                recv_sem=a2a_recv.at[chunk],
                device_id=peer(r),
                device_id_type=MESH,
            ).start()
            return carry

        lax.fori_loop(1, PEERS, body, 0)

    def arrived(chunk):
        _, target = ends(chunk)
        rest = target.at[pl.ds(1, PEERS - 1)]
        pltpu.make_async_copy(rest, rest, a2a_recv.at[chunk]).wait()

    def sent(chunk):
        source, _ = ends(chunk)
        rest = source.at[pl.ds(1, PEERS - 1)]
        pltpu.make_async_copy(rest, rest, a2a_send.at[chunk]).wait()

    def placing(chunk):
        labels = recv0[:, :, FEAT:].reshape(PEERS * ROWS, TAIL).astype(F32)
        w = labels[:, 2 * chunk : 2 * chunk + 1]
        m = labels[:, 2 * chunk + 1 : 2 * chunk + 2]
        plane = lax.div(lax.rem(iota((PEERS * ROWS, 1), 0), ROWS), 2)
        key = m + (plane * 32).astype(F32)
        at = iota((PEERS * ROWS, 256), 1).astype(F32)
        spread = jnp.where(at == key, w, 0.0).T
        place[chunk] = spread.astype(BF16)
        total = jnp.sum(spread[:128], axis=1, keepdims=True)
        part0[4 * chunk : 4 * chunk + 4, :, FEAT:] = jnp.broadcast_to(total, (128, TAIL)).reshape(4, 32, TAIL)

    def accumulate(chunk):
        _, landed = ends(chunk)
        for t in range(FEAT // 256):
            block = landed[:, :, t * 256 : (t + 1) * 256].reshape(PEERS * ROWS, 256)
            numer = jnp.dot(place[chunk], block, preferred_element_type=F32).reshape(2, 4, 32, 256)
            part0[4 * chunk : 4 * chunk + 4, :, t * 256 : (t + 1) * 256] = numer[0]
            part1[4 * chunk : 4 * chunk + 4, :, t * 256 : (t + 1) * 256] = numer[1]

    parts, outs, rings = (part0, part1), (out0, out1), (ring0, ring1)

    def hop(h, way, k):
        return pltpu.make_async_remote_copy(
            src_ref=outs[h].at[way, k],
            dst_ref=rings[h].at[way, k],
            send_sem=ring_send.at[h, way, k],
            recv_sem=ring_recv.at[h, way, k],
            device_id=up if way == 0 else down,
            device_id_type=MESH,
        )

    def received(h, way, k):
        hop(h, way, k).wait_recv()
        if h == 0:
            tail = ring0[way, k, :, FEAT:].astype(jnp.int32).astype(F32)
            high, low = tail[:, 0:1], tail[:, 64:65]
            got[way, k] = jnp.broadcast_to((high * 1024.0 + low) * (1.0 / 512.0), (32, TAIL))
        unit = got[way, k][:, :1] * (LIMIT / LEVELS)
        return rings[h][way, k, :, :FEAT].astype(jnp.int32).astype(F32) * unit

    def step(k, way):
        index = 0 if k == 0 else (2 * k - 1 if way == 0 else 2 * k)
        for h in range(2):
            value = parts[h][index, :, :FEAT]
            joined = k > 1 or (k == 1 and way == 0)
            if joined:
                value = value + received(h, way, k - 1)
            if h == 0:
                weight = part0[index, :, FEAT:]
                if joined:
                    weight = weight + got[way, k - 1]
                units = weight * 512.0
                high = jnp.floor(units * (1.0 / 1024.0))
                low = units - high * 1024.0
                tail = jnp.where(iota((32, TAIL), 1) < 64, high, low)
                out0[way, k, :, FEAT:] = tail.astype(jnp.int32).astype(jnp.int16)
                per = (LEVELS / LIMIT) / jnp.maximum(weight, 0.25)[:, :1]
            level = jnp.floor(value * per + 0.5)
            outs[h][way, k, :, :FEAT] = level.astype(jnp.int32).astype(jnp.int16)
            hop(h, way, k).start()

    def finish(h):
        total = parts[h][15, :, :FEAT]
        for way in range(2):
            total = total + received(h, way, 7)
            if h == 0:
                part0[15, :, FEAT:] += got[way, 7]
        parts[h][15, :, :FEAT] = total

    pl.semaphore_wait(barrier, PEERS + 1)
    pack(0)
    send(0)
    pack(1)
    send(1)
    pack(2)
    pack(3)
    arrived(0)
    send(2)
    placing(0)
    accumulate(0)
    step(0, 0)
    step(1, 0)
    step(1, 1)
    placing(1)
    placing(2)
    placing(3)
    step(2, 0)
    arrived(1)
    send(3)
    accumulate(1)
    step(2, 1)
    step(3, 0)
    step(3, 1)
    step(4, 0)
    arrived(2)
    accumulate(2)
    step(4, 1)
    step(5, 0)
    step(5, 1)
    step(6, 0)
    arrived(3)
    accumulate(3)
    step(6, 1)
    step(7, 0)
    step(7, 1)
    finish(0)

    weight_sum = jnp.maximum(part0[15, :, FEAT:], 1.0)
    for r in range(8):
        t = part0[15, :, r * 128 : (r + 1) * 128] / weight_sum
        for b in range(4):
            tmpl[b, pl.ds(r, 8, stride=16), :] = t[8 * b : 8 * b + 8]
    finish(1)
    for r in range(8):
        t = part1[15, :, r * 128 : (r + 1) * 128] / weight_sum
        for b in range(4):
            tmpl[b, pl.ds(r + 8, 8, stride=16), :] = t[8 * b : 8 * b + 8]
    for b in range(4):
        window[0:BAND, 128 * b : 128 * (b + 1)] = tmpl[b].astype(BF16)

    below = pltpu.make_async_remote_copy(
        src_ref=window.at[pl.ds(BAND - ROWS, ROWS)], dst_ref=halo.at[0],
        send_sem=halo_send.at[0], recv_sem=halo_recv.at[0],
        device_id=(p, lax.rem(x + 1, NX)), device_id_type=MESH,
    )
    above = pltpu.make_async_remote_copy(
        src_ref=window.at[pl.ds(0, ROWS)], dst_ref=halo.at[1],
        send_sem=halo_send.at[1], recv_sem=halo_recv.at[1],
        device_id=(p, lax.rem(x + NX - 1, NX)), device_id_type=MESH,
    )
    below.start()
    above.start()

    stamp_rows = jnp.where(lax.div(iota((BAND, 8), 0), 16) == iota((BAND, 8), 1), 1.0, 0.0)
    stamp_cols = jnp.where(lax.div(iota((32, WIDTH), 1), 16) == iota((32, WIDTH), 0), 1.0, 0.0)
    good = jnp.where(good_ref[0] == 1, 1.0, 0.0)
    mask = jnp.dot(jnp.dot(stamp_rows, good, preferred_element_type=F32), stamp_cols, preferred_element_type=F32)
    design[:, 18] = mask.astype(BF16).reshape(8, ROWS, WIDTH)
    design[:, 19] = (science_ref[0].astype(F32) * mask).astype(BF16).reshape(8, ROWS, WIDTH)
    window[BAND + 2 * ROWS :, :] = jnp.zeros((256 - BAND - 2 * ROWS, WIDTH), BF16)
    load_vert.wait()
    load_horiz.wait()

    below.wait_recv()
    above.wait_recv()
    window[BAND : BAND + ROWS, :] = jnp.where(x > 0, halo[0].astype(F32), 0.0).astype(BF16)
    window[BAND + ROWS : BAND + 2 * ROWS, :] = jnp.where(x < NX - 1, halo[1].astype(F32), 0.0).astype(BF16)

    for f in range(3):
        rows = slice(f * 3 * BAND, (f + 1) * 3 * BAND)
        vimg[rows] = jnp.dot(vert[rows], window[...], preferred_element_type=F32).astype(BF16)

    for g in range(3):
        for i in range(3):
            count = (3 - i) * BAND
            image = jnp.dot(
                vimg[g * 3 * BAND : g * 3 * BAND + count], horiz[g * 3 + i], preferred_element_type=F32
            )
            for j in range(3 - i):
                k = g * 6 + BASIS_PAIRS.index((i, j))
                part = image[j * BAND : (j + 1) * BAND].astype(BF16).astype(F32) * mask
                design[:, k] = part.astype(BF16).reshape(8, ROWS, WIDTH)

    def product(q, total):
        block = design[q].reshape(20 * ROWS, WIDTH)
        return total + lax.dot_general(
            block, block, (((1,), (1,)), ((), ())), preferred_element_type=F32
        )

    total = lax.fori_loop(0, 8, product, jnp.zeros((20 * ROWS, 20 * ROWS), F32))
    same = lax.rem(iota((320, 320), 0), ROWS) == lax.rem(iota((320, 320), 1), ROWS)
    total = jnp.sum(jnp.where(same, total, 0.0).reshape(20, ROWS, 320), axis=1)
    fold = jnp.where(lax.div(iota((320, 128), 0), ROWS) == iota((320, 128), 1), 1.0, 0.0)
    normal = jnp.dot(total, fold, preferred_element_type=F32, precision=lax.Precision.HIGHEST)
    normal = jnp.concatenate([normal, jnp.zeros((4, 128), F32)], axis=0)
    gram_mine[...] = normal
    gram_all[x] = normal

    shares = [
        pltpu.make_async_remote_copy(
            src_ref=gram_mine, dst_ref=gram_all.at[x],
            send_sem=gram_send.at[d - 1], recv_sem=gram_recv.at[d - 1],
            device_id=(p, lax.rem(x + d, NX)), device_id_type=MESH,
        )
        for d in range(1, NX)
    ]
    for share in shares:
        share.start()
    for share in shares:
        share.wait_recv()
    normal = gram_all[0] + gram_all[1] + gram_all[2] + gram_all[3]

    rows = iota((24, 128), 0)
    lanes = iota((24, 128), 1)
    diagonal = (rows == lanes) & (rows < 19)
    system = normal + jnp.where(diagonal, RIDGE * normal, 0.0)
    for k in range(19):
        pivot_row = system[k : k + 1] / system[k : k + 1, k : k + 1]
        column = jnp.where(rows[:, :1] == k, 0.0, system[:, k : k + 1])
        system = system - column * pivot_row
    rhs = system[:, 19:20]
    lead = jnp.sum(jnp.where(diagonal, system, 0.0), axis=1, keepdims=True)
    solved = rhs / jnp.where(rows[:, :1] < 19, lead, 1.0)
    coef_ref[...] = jnp.sum(jnp.where(diagonal, solved, 0.0), axis=0, keepdims=True)[:, :19]

    def model(q, carry):
        value = design[q, 19].astype(F32)
        for k in range(19):
            value = value - solved[k : k + 1] * design[q, k].astype(F32)
        diff_ref[0, pl.ds(q * ROWS, ROWS), :] = value.astype(BF16)
        return carry

    lax.fori_loop(0, 8, model, 0)

    for chunk in range(4):
        sent(chunk)
    for h in range(2):
        for way in range(2):
            for k in range(8):
                if k > 0 or way == 0:
                    hop(h, way, k).wait_send()
    below.wait_send()
    above.wait_send()
    for share in shares:
        share.wait_send()


def shards(pieces, piece_slot, piece_cell, weights, science, good_stamps):
    vmem = pl.BlockSpec(memory_space=pltpu.VMEM)
    anywhere = pl.BlockSpec(memory_space=pl.ANY)
    dma = pltpu.SemaphoreType.DMA
    return pl.pallas_call(
        kernel,
        out_shape=(
            jax.ShapeDtypeStruct((1, BAND, WIDTH), BF16),
            jax.ShapeDtypeStruct((1, 19), F32),
        ),
        in_specs=[vmem] * 5 + [anywhere] * 3,
        out_specs=(vmem, vmem),
        scratch_shapes=[
            pltpu.VMEM((512, 2048), BF16),
            pltpu.VMEM((9 * BAND, 256), BF16),
            pltpu.VMEM((9, WIDTH, WIDTH), BF16),
            pltpu.VMEM((4, 2, 128, 512), BF16),
            pltpu.VMEM((PEERS, ROWS, FEAT + TAIL), BF16),
            pltpu.VMEM((3, PEERS, ROWS, FEAT), BF16),
            pltpu.VMEM((PEERS, ROWS, FEAT + TAIL), BF16),
            pltpu.VMEM((3, PEERS, ROWS, FEAT), BF16),
            pltpu.VMEM((4, 256, PEERS * ROWS), BF16),
            pltpu.VMEM((NZ, 32, FEAT + TAIL), F32),
            pltpu.VMEM((NZ, 32, FEAT), F32),
            pltpu.VMEM((2, 8, 32, FEAT + TAIL), jnp.int16),
            pltpu.VMEM((2, 8, 32, FEAT), jnp.int16),
            pltpu.VMEM((2, 8, 32, FEAT + TAIL), jnp.int16),
            pltpu.VMEM((2, 8, 32, FEAT), jnp.int16),
            pltpu.VMEM((2, 8, 32, TAIL), F32),
            pltpu.VMEM((4, BAND, 128), F32),
            pltpu.VMEM((256, WIDTH), BF16),
            pltpu.VMEM((2, ROWS, WIDTH), BF16),
            pltpu.VMEM((9 * BAND, WIDTH), BF16),
            pltpu.VMEM((8, 20, ROWS, WIDTH), BF16),
            pltpu.VMEM((24, 128), F32),
            pltpu.VMEM((NX, 24, 128), F32),
            dma((3,)),
            dma((4,)),
            dma((4,)),
            dma((2, 2, 8)),
            dma((2, 2, 8)),
            dma((2,)),
            dma((2,)),
            dma((3,)),
            dma((3,)),
        ],
        compiler_params=pltpu.CompilerParams(
            collective_id=0, has_side_effects=True, vmem_limit_bytes=56 * 2**20
        ),
    )(
        piece_slot[0], piece_cell[0], weights[0], science, good_stamps, pieces,
        jnp.asarray(vertical_matrix()), jnp.asarray(horizontal_matrix()),
    )


def solution(mesh):
    in_specs = (
        P("patch", "sub", None, None),
        P("patch", "sub", None),
        P("patch", "sub", None),
        P("patch", "sub", None),
        P("patch", "sub", None),
        P("patch", "sub", None),
    )
    out_specs = (P("patch", "sub", None), P("patch", None))
    return jax.shard_map(shards, mesh=mesh, in_specs=in_specs, out_specs=out_specs, check_vma=False)
```

```python
import functools
import math

import jax
import jax.numpy as jnp
import numpy as np
from jax import lax
from jax.experimental import pallas as pl
from jax.experimental.pallas import tpu as pltpu
from jax.sharding import PartitionSpec as P

MESH = pl.DeviceIdType.MESH
F32 = jnp.float32
BF16 = jnp.bfloat16

NX, NY, NZ, NC = 4, 4, 16, 2
PEERS = NX * NY * NC
ROWS = 16
BAND = 128
WIDTH = 512
KSIZE = 23
DEGREE = 2
HALF = 11
SIGMAS = (0.75, 1.5, 3.0)
RIDGE = 0.1
BASIS_PAIRS = ((0, 0), (1, 0), (0, 1), (2, 0), (1, 1), (0, 2))
FEAT = 1024
TAIL = 128
LIMIT = 10.0
LEVELS = 32700.0


def filter_table():
    result = []
    for sigma in SIGMAS:
        for power in range(DEGREE + 1):
            entries = []
            for offset in range(KSIZE):
                position = float(offset - HALF)
                entries.append(
                    math.exp(-position * position / (2.0 * sigma * sigma))
                    * (position / sigma) ** power
                )
            norm_value = math.sqrt(sum([entry * entry for entry in entries]))
            result.append([entry / norm_value for entry in entries])
    return np.array(result, dtype=np.float32)


def vertical_matrix():
    filters = filter_table()
    matrix = np.zeros((9, BAND, 256), np.float32)
    for row in range(BAND):
        for v in range(-HALF, HALF + 1):
            source = row + v
            if source < 0:
                column = BAND + ROWS + source
            elif source >= BAND:
                column = BAND + ROWS + source - BAND
            else:
                column = source
            matrix[:, row, column] = filters[:, v + HALF]
    return matrix.reshape(9 * BAND, 256).astype(jnp.bfloat16)


def horizontal_matrix():
    filters = filter_table()
    matrix = np.zeros((9, WIDTH, WIDTH), np.float32)
    for u in range(-HALF, HALF + 1):
        x = np.arange(max(0, -u), min(WIDTH, WIDTH - u))
        matrix[:, x + u, x] = filters[:, u + HALF][:, None]
    return matrix.astype(jnp.bfloat16)


def iota(shape, axis):
    return lax.broadcasted_iota(jnp.int32, shape, axis)


def kernel(
    slot_ref, cell_ref, weight_ref, science_ref, good_ref, pieces_hbm, vert_hbm, horiz_hbm,
    diff_ref, coef_ref,
    pieces, vert, horiz, onehot, send0, send1, recv0, recv1, place,
    part0, part1, out0, out1, ring0, ring1, got, tmpl, window, halo, vimg, design, gram_mine, gram_all,
    local_sem, a2a_send, a2a_recv, ring_send, ring_recv, halo_send, halo_recv, gram_send, gram_recv,
):
    p = lax.axis_index("patch")
    x = lax.axis_index("sub")
    c = lax.rem(p, NC)
    z = lax.rem(lax.div(p, NC), NZ)
    y = lax.div(p, NC * NZ)

    def patch_of(yy, zz, cc):
        return (yy * NZ + zz) * NC + cc

    load_pieces = pltpu.make_async_copy(pieces_hbm.at[0, 0], pieces, local_sem.at[0])
    load_vert = pltpu.make_async_copy(vert_hbm, vert, local_sem.at[1])
    load_horiz = pltpu.make_async_copy(horiz_hbm, horiz, local_sem.at[2])
    load_pieces.start()

    barrier = pltpu.get_barrier_semaphore()

    def peer(r):
        dy = lax.div(r, NC * NX)
        dc = lax.rem(lax.div(r, NX), NC)
        dx = lax.rem(r, NX)
        return (
            patch_of(lax.rem(y + dy, NY), z, lax.rem(c + dc, NC)),
            lax.rem(x + dx, NX),
        )

    up = (patch_of(y, lax.rem(z + 1, NZ), c), x)
    down = (patch_of(y, lax.rem(z + NZ - 1, NZ), c), x)

    def greet(r, carry):
        pl.semaphore_signal(barrier, inc=1, device_id=peer(r), device_id_type=MESH)
        return carry

    lax.fori_loop(1, PEERS, greet, 0)
    pl.semaphore_signal(barrier, inc=1, device_id=up, device_id_type=MESH)
    pl.semaphore_signal(barrier, inc=1, device_id=down, device_id_type=MESH)

    slots = slot_ref[0]
    cells = cell_ref[0]
    weights = weight_ref[0].astype(F32)
    marks = (lax.rem(cells, 4) * 8 + lax.div(cells, 4)).astype(F32)
    row = iota((128, 1), 0)
    peer_in = lax.rem(lax.div(row, 8), NC * NX)
    cc = lax.rem(c + lax.div(peer_in, NX), NC)
    xx = lax.rem(x + lax.rem(peer_in, NX), NX)
    within = lax.rem(row, 8)
    base = []
    for chunk in range(4):
        j = lax.div(within, 2) + 4 * chunk
        half = lax.div(j + 1, 2)
        off = jnp.where(lax.rem(j, 2) == 1, 8 - half, half - 8)
        zz = lax.rem(z + off + NZ, NZ)
        base.append(zz * 16 + cc * 8 + xx * 2 + lax.rem(within, 2))
    lane = iota((128, TAIL), 1)

    def both(a, b, width):
        pair = [t.reshape(16, 8, width) for t in (a, b)]
        return jnp.concatenate(pair, axis=1).astype(BF16)

    def select(two, carry):
        yy = lax.rem(y + 2 * two + lax.div(row, 64), NY) * 256
        tail = jnp.zeros((128, TAIL), F32)
        for chunk in range(4):
            hit = slots == base[chunk] + yy
            onehot[chunk, two] = jnp.where(hit, 1.0, 0.0).astype(BF16)
            w = jnp.sum(jnp.where(hit, weights, 0.0), axis=1, keepdims=True)
            m = jnp.sum(jnp.where(hit, marks, 0.0), axis=1, keepdims=True)
            tail = jnp.where(lane == 2 * chunk, w, jnp.where(lane == 2 * chunk + 1, m, tail))
        send0[pl.ds(two * 16, 16), :, FEAT:] = both(tail, tail, TAIL)
        return carry

    lax.fori_loop(0, 2, select, 0)
    recv0[0, :, FEAT:] = send0[0, :, FEAT:]

    load_pieces.wait()
    load_vert.start()
    load_horiz.start()

    def pack(chunk):
        def body(two, carry):
            a, b = (
                jnp.dot(
                    onehot[chunk, two], pieces[:, h * FEAT : (h + 1) * FEAT], preferred_element_type=F32
                )
                for h in range(2)
            )
            picked = both(a, b, FEAT)
            if chunk == 0:
                send0[pl.ds(two * 16, 16), :, :FEAT] = picked

                @pl.when(two == 0)
                def _():
                    recv0[0, :, :FEAT] = picked[0]
            else:
                send1[chunk - 1, pl.ds(two * 16, 16)] = picked

                @pl.when(two == 0)
                def _():
                    recv1[chunk - 1, 0] = picked[0]
            return carry

        lax.fori_loop(0, 2, body, 0)

    def ends(chunk):
        if chunk == 0:
            return send0, recv0
        return send1.at[chunk - 1], recv1.at[chunk - 1]

    def send(chunk):
        source, target = ends(chunk)

        def body(i, carry):
            r = lax.rem(i * 11, PEERS)
            pltpu.make_async_remote_copy(
                src_ref=source.at[r],
                dst_ref=target.at[r],
                send_sem=a2a_send.at[chunk],
                recv_sem=a2a_recv.at[chunk],
                device_id=peer(r),
                device_id_type=MESH,
            ).start()
            return carry

        lax.fori_loop(1, PEERS, body, 0)

    def arrived(chunk):
        _, target = ends(chunk)
        rest = target.at[pl.ds(1, PEERS - 1)]
        pltpu.make_async_copy(rest, rest, a2a_recv.at[chunk]).wait()

    def sent(chunk):
        source, _ = ends(chunk)
        rest = source.at[pl.ds(1, PEERS - 1)]
        pltpu.make_async_copy(rest, rest, a2a_send.at[chunk]).wait()

    def placing(chunk):
        labels = recv0[:, :, FEAT:].reshape(PEERS * ROWS, TAIL).astype(F32)
        w = labels[:, 2 * chunk : 2 * chunk + 1]
        m = labels[:, 2 * chunk + 1 : 2 * chunk + 2]
        plane = lax.div(lax.rem(iota((PEERS * ROWS, 1), 0), ROWS), 2)
        key = m + (plane * 32).astype(F32)
        at = iota((PEERS * ROWS, 256), 1).astype(F32)
        spread = jnp.where(at == key, w, 0.0).T
        place[chunk] = spread.astype(BF16)
        total = jnp.sum(spread[:128], axis=1, keepdims=True)
        part0[4 * chunk : 4 * chunk + 4, :, FEAT:] = jnp.broadcast_to(total, (128, TAIL)).reshape(4, 32, TAIL)

    def accumulate(chunk):
        _, landed = ends(chunk)
        for t in range(FEAT // 256):
            block = landed[:, :, t * 256 : (t + 1) * 256].reshape(PEERS * ROWS, 256)
            numer = jnp.dot(place[chunk], block, preferred_element_type=F32).reshape(2, 4, 32, 256)
            part0[4 * chunk : 4 * chunk + 4, :, t * 256 : (t + 1) * 256] = numer[0]
            part1[4 * chunk : 4 * chunk + 4, :, t * 256 : (t + 1) * 256] = numer[1]

    parts, outs, rings = (part0, part1), (out0, out1), (ring0, ring1)

    def hop(h, way, k):
        return pltpu.make_async_remote_copy(
            src_ref=outs[h].at[way, k],
            dst_ref=rings[h].at[way, k],
            send_sem=ring_send.at[h, way, k],
            recv_sem=ring_recv.at[h, way, k],
            device_id=up if way == 0 else down,
            device_id_type=MESH,
        )

    def received(h, way, k):
        hop(h, way, k).wait_recv()
        if h == 0:
            tail = ring0[way, k, :, FEAT:].astype(jnp.int32).astype(F32)
            high, low = tail[:, 0:1], tail[:, 64:65]
            got[way, k] = jnp.broadcast_to((high * 1024.0 + low) * (1.0 / 512.0), (32, TAIL))
        unit = got[way, k][:, :1] * (LIMIT / LEVELS)
        return rings[h][way, k, :, :FEAT].astype(jnp.int32).astype(F32) * unit

    def step(k, way):
        index = 0 if k == 0 else (2 * k - 1 if way == 0 else 2 * k)
        for h in range(2):
            value = parts[h][index, :, :FEAT]
            joined = k > 1 or (k == 1 and way == 0)
            if joined:
                value = value + received(h, way, k - 1)
            if h == 0:
                weight = part0[index, :, FEAT:]
                if joined:
                    weight = weight + got[way, k - 1]
                units = weight * 512.0
                high = jnp.floor(units * (1.0 / 1024.0))
                low = units - high * 1024.0
                tail = jnp.where(iota((32, TAIL), 1) < 64, high, low)
                out0[way, k, :, FEAT:] = tail.astype(jnp.int32).astype(jnp.int16)
                per = (LEVELS / LIMIT) / jnp.maximum(weight, 0.25)[:, :1]
            level = jnp.floor(value * per + 0.5)
            outs[h][way, k, :, :FEAT] = level.astype(jnp.int32).astype(jnp.int16)
            hop(h, way, k).start()

    def finish(h):
        total = parts[h][15, :, :FEAT]
        for way in range(2):
            total = total + received(h, way, 7)
            if h == 0:
                part0[15, :, FEAT:] += got[way, 7]
        parts[h][15, :, :FEAT] = total

    pack(0)
    pl.semaphore_wait(barrier, PEERS + 1)
    send(0)
    pack(1)
    send(1)
    pack(2)
    pack(3)
    arrived(0)
    send(2)
    placing(0)
    accumulate(0)
    step(0, 0)
    step(1, 0)
    step(1, 1)
    placing(1)
    placing(2)
    placing(3)
    step(2, 0)
    arrived(1)
    send(3)
    accumulate(1)
    step(2, 1)
    step(3, 0)
    step(3, 1)
    step(4, 0)
    arrived(2)
    accumulate(2)
    step(4, 1)
    step(5, 0)
    step(5, 1)
    step(6, 0)
    arrived(3)
    accumulate(3)
    step(6, 1)
    step(7, 0)
    step(7, 1)
    finish(0)

    weight_sum = jnp.maximum(part0[15, :, FEAT:], 1.0)
    for r in range(8):
        t = part0[15, :, r * 128 : (r + 1) * 128] / weight_sum
        for b in range(4):
            tmpl[b, pl.ds(r, 8, stride=16), :] = t[8 * b : 8 * b + 8]
    finish(1)
    for r in range(8):
        t = part1[15, :, r * 128 : (r + 1) * 128] / weight_sum
        for b in range(4):
            tmpl[b, pl.ds(r + 8, 8, stride=16), :] = t[8 * b : 8 * b + 8]
    for b in range(4):
        window[0:BAND, 128 * b : 128 * (b + 1)] = tmpl[b].astype(BF16)

    below = pltpu.make_async_remote_copy(
        src_ref=window.at[pl.ds(BAND - ROWS, ROWS)], dst_ref=halo.at[0],
        send_sem=halo_send.at[0], recv_sem=halo_recv.at[0],
        device_id=(p, lax.rem(x + 1, NX)), device_id_type=MESH,
    )
    above = pltpu.make_async_remote_copy(
        src_ref=window.at[pl.ds(0, ROWS)], dst_ref=halo.at[1],
        send_sem=halo_send.at[1], recv_sem=halo_recv.at[1],
        device_id=(p, lax.rem(x + NX - 1, NX)), device_id_type=MESH,
    )
    below.start()
    above.start()

    stamp_rows = jnp.where(lax.div(iota((BAND, 8), 0), 16) == iota((BAND, 8), 1), 1.0, 0.0)
    stamp_cols = jnp.where(lax.div(iota((32, WIDTH), 1), 16) == iota((32, WIDTH), 0), 1.0, 0.0)
    good = jnp.where(good_ref[0] == 1, 1.0, 0.0)
    mask = jnp.dot(jnp.dot(stamp_rows, good, preferred_element_type=F32), stamp_cols, preferred_element_type=F32)
    design[:, 18] = mask.astype(BF16).reshape(8, ROWS, WIDTH)
    design[:, 19] = (science_ref[0].astype(F32) * mask).astype(BF16).reshape(8, ROWS, WIDTH)
    window[BAND + 2 * ROWS :, :] = jnp.zeros((256 - BAND - 2 * ROWS, WIDTH), BF16)
    load_vert.wait()
    load_horiz.wait()

    below.wait_recv()
    above.wait_recv()
    window[BAND : BAND + ROWS, :] = jnp.where(x > 0, halo[0].astype(F32), 0.0).astype(BF16)
    window[BAND + ROWS : BAND + 2 * ROWS, :] = jnp.where(x < NX - 1, halo[1].astype(F32), 0.0).astype(BF16)

    for f in range(3):
        rows = slice(f * 3 * BAND, (f + 1) * 3 * BAND)
        vimg[rows] = jnp.dot(vert[rows], window[...], preferred_element_type=F32).astype(BF16)

    for g in range(3):
        for i in range(3):
            count = (3 - i) * BAND
            image = jnp.dot(
                vimg[g * 3 * BAND : g * 3 * BAND + count], horiz[g * 3 + i], preferred_element_type=F32
            )
            for j in range(3 - i):
                k = g * 6 + BASIS_PAIRS.index((i, j))
                part = image[j * BAND : (j + 1) * BAND].astype(BF16).astype(F32) * mask
                design[:, k] = part.astype(BF16).reshape(8, ROWS, WIDTH)

    def product(q, sums):
        block = design[q].reshape(20 * ROWS, WIDTH)
        corner = block[16 * ROWS :]
        return tuple(
            total + lax.dot_general(a, b, (((1,), (1,)), ((), ())), preferred_element_type=F32)
            for total, a, b in zip(sums, (block, corner), (block[: 16 * ROWS], corner))
        )

    sums = lax.fori_loop(0, 8, product, (jnp.zeros((320, 256), F32), jnp.zeros((64, 64), F32)))

    def folded(total, first):
        high, wide = total.shape
        same = lax.rem(iota(total.shape, 0), ROWS) == lax.rem(iota(total.shape, 1), ROWS)
        total = jnp.sum(jnp.where(same, total, 0.0).reshape(high // ROWS, ROWS, wide), axis=1)
        fold = lax.div(iota((wide, 128), 0), ROWS) + first == iota((wide, 128), 1)
        fold = jnp.where(fold, 1.0, 0.0)
        return jnp.dot(total, fold, preferred_element_type=F32, precision=lax.Precision.HIGHEST)

    def blank(count):
        return jnp.zeros((count, 128), F32)

    left, right = folded(sums[0], 0), folded(sums[1], 16)
    mirror = jnp.concatenate([blank(16), left[16:20], blank(108)], axis=0).T[:24]
    normal = (
        jnp.concatenate([left, blank(4)], axis=0)
        + jnp.concatenate([blank(16), right, blank(4)], axis=0)
        + mirror
    )
    gram_mine[...] = normal
    gram_all[x] = normal

    shares = [
        pltpu.make_async_remote_copy(
            src_ref=gram_mine, dst_ref=gram_all.at[x],
            send_sem=gram_send.at[d - 1], recv_sem=gram_recv.at[d - 1],
            device_id=(p, lax.rem(x + d, NX)), device_id_type=MESH,
        )
        for d in range(1, NX)
    ]
    for share in shares:
        share.start()
    for share in shares:
        share.wait_recv()
    normal = gram_all[0] + gram_all[1] + gram_all[2] + gram_all[3]

    rows = iota((24, 128), 0)
    lanes = iota((24, 128), 1)
    diagonal = (rows == lanes) & (rows < 19)
    system = normal + jnp.where(diagonal, RIDGE * normal, 0.0)
    for k in range(19):
        pivot_row = system[k : k + 1] / system[k : k + 1, k : k + 1]
        column = jnp.where(rows[:, :1] == k, 0.0, system[:, k : k + 1])
        system = system - column * pivot_row
    rhs = system[:, 19:20]
    lead = jnp.sum(jnp.where(diagonal, system, 0.0), axis=1, keepdims=True)
    solved = rhs / jnp.where(rows[:, :1] < 19, lead, 1.0)
    coef_ref[...] = jnp.sum(jnp.where(diagonal, solved, 0.0), axis=0, keepdims=True)[:, :19]

    def model(q, carry):
        value = design[q, 19].astype(F32)
        for k in range(19):
            value = value - solved[k : k + 1] * design[q, k].astype(F32)
        diff_ref[0, pl.ds(q * ROWS, ROWS), :] = value.astype(BF16)
        return carry

    lax.fori_loop(0, 8, model, 0)

    for chunk in range(4):
        sent(chunk)
    for h in range(2):
        for way in range(2):
            for k in range(8):
                if k > 0 or way == 0:
                    hop(h, way, k).wait_send()
    below.wait_send()
    above.wait_send()
    for share in shares:
        share.wait_send()


def shards(pieces, piece_slot, piece_cell, weights, science, good_stamps):
    vmem = pl.BlockSpec(memory_space=pltpu.VMEM)
    anywhere = pl.BlockSpec(memory_space=pl.ANY)
    dma = pltpu.SemaphoreType.DMA
    return pl.pallas_call(
        kernel,
        out_shape=(
            jax.ShapeDtypeStruct((1, BAND, WIDTH), BF16),
            jax.ShapeDtypeStruct((1, 19), F32),
        ),
        in_specs=[vmem] * 5 + [anywhere] * 3,
        out_specs=(vmem, vmem),
        scratch_shapes=[
            pltpu.VMEM((512, 2048), BF16),
            pltpu.VMEM((9 * BAND, 256), BF16),
            pltpu.VMEM((9, WIDTH, WIDTH), BF16),
            pltpu.VMEM((4, 2, 128, 512), BF16),
            pltpu.VMEM((PEERS, ROWS, FEAT + TAIL), BF16),
            pltpu.VMEM((3, PEERS, ROWS, FEAT), BF16),
            pltpu.VMEM((PEERS, ROWS, FEAT + TAIL), BF16),
            pltpu.VMEM((3, PEERS, ROWS, FEAT), BF16),
            pltpu.VMEM((4, 256, PEERS * ROWS), BF16),
            pltpu.VMEM((NZ, 32, FEAT + TAIL), F32),
            pltpu.VMEM((NZ, 32, FEAT), F32),
            pltpu.VMEM((2, 8, 32, FEAT + TAIL), jnp.int16),
            pltpu.VMEM((2, 8, 32, FEAT), jnp.int16),
            pltpu.VMEM((2, 8, 32, FEAT + TAIL), jnp.int16),
            pltpu.VMEM((2, 8, 32, FEAT), jnp.int16),
            pltpu.VMEM((2, 8, 32, TAIL), F32),
            pltpu.VMEM((4, BAND, 128), F32),
            pltpu.VMEM((256, WIDTH), BF16),
            pltpu.VMEM((2, ROWS, WIDTH), BF16),
            pltpu.VMEM((9 * BAND, WIDTH), BF16),
            pltpu.VMEM((8, 20, ROWS, WIDTH), BF16),
            pltpu.VMEM((24, 128), F32),
            pltpu.VMEM((NX, 24, 128), F32),
            dma((3,)),
            dma((4,)),
            dma((4,)),
            dma((2, 2, 8)),
            dma((2, 2, 8)),
            dma((2,)),
            dma((2,)),
            dma((3,)),
            dma((3,)),
        ],
        compiler_params=pltpu.CompilerParams(
            collective_id=0, has_side_effects=True, vmem_limit_bytes=56 * 2**20
        ),
    )(
        piece_slot[0], piece_cell[0], weights[0], science, good_stamps, pieces,
        jnp.asarray(vertical_matrix()), jnp.asarray(horizontal_matrix()),
    )


def solution(mesh):
    in_specs = (
        P("patch", "sub", None, None),
        P("patch", "sub", None),
        P("patch", "sub", None),
        P("patch", "sub", None),
        P("patch", "sub", None),
        P("patch", "sub", None),
    )
    out_specs = (P("patch", "sub", None), P("patch", None))
    return jax.shard_map(shards, mesh=mesh, in_specs=in_specs, out_specs=out_specs, check_vma=False)
```

```python
import functools
import math

import jax
import jax.numpy as jnp
import numpy as np
from jax import lax
from jax.experimental import pallas as pl
from jax.experimental.pallas import tpu as pltpu
from jax.sharding import PartitionSpec as P

MESH = pl.DeviceIdType.MESH
F32 = jnp.float32
BF16 = jnp.bfloat16

NX, NY, NZ, NC = 4, 4, 16, 2
PEERS = NX * NY * NC
ROWS = 16
BAND = 128
WIDTH = 512
KSIZE = 23
DEGREE = 2
HALF = 11
SIGMAS = (0.75, 1.5, 3.0)
RIDGE = 0.1
BASIS_PAIRS = ((0, 0), (1, 0), (0, 1), (2, 0), (1, 1), (0, 2))
FEAT = 1024
TAIL = 128
LIMIT = 10.0
LEVELS = 32700.0


def filter_table():
    result = []
    for sigma in SIGMAS:
        for power in range(DEGREE + 1):
            entries = []
            for offset in range(KSIZE):
                position = float(offset - HALF)
                entries.append(
                    math.exp(-position * position / (2.0 * sigma * sigma))
                    * (position / sigma) ** power
                )
            norm_value = math.sqrt(sum([entry * entry for entry in entries]))
            result.append([entry / norm_value for entry in entries])
    return np.array(result, dtype=np.float32)


def vertical_matrix():
    filters = filter_table()
    matrix = np.zeros((9, BAND, 256), np.float32)
    for row in range(BAND):
        for v in range(-HALF, HALF + 1):
            source = row + v
            if source < 0:
                column = BAND + ROWS + source
            elif source >= BAND:
                column = BAND + ROWS + source - BAND
            else:
                column = source
            matrix[:, row, column] = filters[:, v + HALF]
    return matrix.reshape(9 * BAND, 256).astype(jnp.bfloat16)


def horizontal_matrix():
    filters = filter_table()
    matrix = np.zeros((9, WIDTH, WIDTH), np.float32)
    for u in range(-HALF, HALF + 1):
        x = np.arange(max(0, -u), min(WIDTH, WIDTH - u))
        matrix[:, x + u, x] = filters[:, u + HALF][:, None]
    return matrix.astype(jnp.bfloat16)


def iota(shape, axis):
    return lax.broadcasted_iota(jnp.int32, shape, axis)


def kernel(
    slot_ref, cell_ref, weight_ref, science_ref, good_ref, pieces_hbm, vert_hbm, horiz_hbm,
    diff_ref, coef_ref,
    pieces, vert, horiz, onehot, send0, send1, recv0, recv1, place,
    part0, part1, out0, out1, ring0, ring1, got, tmpl, window, halo, vimg, design, gram_mine, gram_all,
    local_sem, a2a_send, a2a_recv, ring_send, ring_recv, halo_send, halo_recv, gram_send, gram_recv,
):
    p = lax.axis_index("patch")
    x = lax.axis_index("sub")
    c = lax.rem(p, NC)
    z = lax.rem(lax.div(p, NC), NZ)
    y = lax.div(p, NC * NZ)

    def patch_of(yy, zz, cc):
        return (yy * NZ + zz) * NC + cc

    load_pieces = pltpu.make_async_copy(pieces_hbm.at[0, 0], pieces, local_sem.at[0])
    load_vert = pltpu.make_async_copy(vert_hbm, vert, local_sem.at[1])
    load_horiz = pltpu.make_async_copy(horiz_hbm, horiz, local_sem.at[2])
    load_pieces.start()

    barrier = pltpu.get_barrier_semaphore()

    y_at = [patch_of(lax.rem(y + dy, NY), z, 0) for dy in range(NY)]
    c_at = [lax.rem(c + dc, NC) for dc in range(NC)]
    x_at = [lax.rem(x + dx, NX) for dx in range(NX)]

    def peer(r):
        dy, dc, dx = r // (NC * NX), r // NX % NC, r % NX
        return (y_at[dy] + c_at[dc], x_at[dx])

    up = (patch_of(y, lax.rem(z + 1, NZ), c), x)
    down = (patch_of(y, lax.rem(z + NZ - 1, NZ), c), x)

    for r in range(1, PEERS):
        pl.semaphore_signal(barrier, inc=1, device_id=peer(r), device_id_type=MESH)
    pl.semaphore_signal(barrier, inc=1, device_id=up, device_id_type=MESH)
    pl.semaphore_signal(barrier, inc=1, device_id=down, device_id_type=MESH)

    slots = slot_ref[0]
    cells = cell_ref[0]
    weights = weight_ref[0].astype(F32)
    marks = (lax.rem(cells, 4) * 8 + lax.div(cells, 4)).astype(F32)
    row = iota((128, 1), 0)
    peer_in = lax.rem(lax.div(row, 8), NC * NX)
    cc = lax.rem(c + lax.div(peer_in, NX), NC)
    xx = lax.rem(x + lax.rem(peer_in, NX), NX)
    within = lax.rem(row, 8)
    base = []
    for chunk in range(4):
        j = lax.div(within, 2) + 4 * chunk
        half = lax.div(j + 1, 2)
        off = jnp.where(lax.rem(j, 2) == 1, 8 - half, half - 8)
        zz = lax.rem(z + off + NZ, NZ)
        base.append(zz * 16 + cc * 8 + xx * 2 + lax.rem(within, 2))
    lane = iota((128, TAIL), 1)

    def both(a, b, width):
        pair = [t.reshape(16, 8, width) for t in (a, b)]
        return jnp.concatenate(pair, axis=1).astype(BF16)

    def select(two, carry):
        yy = lax.rem(y + 2 * two + lax.div(row, 64), NY) * 256
        tail = jnp.zeros((128, TAIL), F32)
        for chunk in range(4):
            hit = slots == base[chunk] + yy
            onehot[chunk, two] = jnp.where(hit, 1.0, 0.0).astype(BF16)
            w = jnp.sum(jnp.where(hit, weights, 0.0), axis=1, keepdims=True)
            m = jnp.sum(jnp.where(hit, marks, 0.0), axis=1, keepdims=True)
            tail = jnp.where(lane == 2 * chunk, w, jnp.where(lane == 2 * chunk + 1, m, tail))
        send0[pl.ds(two * 16, 16), :, FEAT:] = both(tail, tail, TAIL)
        return carry

    lax.fori_loop(0, 2, select, 0)
    recv0[0, :, FEAT:] = send0[0, :, FEAT:]

    load_pieces.wait()
    load_vert.start()
    load_horiz.start()

    def pack(chunk):
        def body(two, carry):
            a, b = (
                jnp.dot(
                    onehot[chunk, two], pieces[:, h * FEAT : (h + 1) * FEAT], preferred_element_type=F32
                )
                for h in range(2)
            )
            picked = both(a, b, FEAT)
            if chunk == 0:
                send0[pl.ds(two * 16, 16), :, :FEAT] = picked

                @pl.when(two == 0)
                def _():
                    recv0[0, :, :FEAT] = picked[0]
            else:
                send1[chunk - 1, pl.ds(two * 16, 16)] = picked

                @pl.when(two == 0)
                def _():
                    recv1[chunk - 1, 0] = picked[0]
            return carry

        lax.fori_loop(0, 2, body, 0)

    def ends(chunk):
        if chunk == 0:
            return send0, recv0
        return send1.at[chunk - 1], recv1.at[chunk - 1]

    def send(chunk):
        source, target = ends(chunk)

        for i in range(1, PEERS):
            r = i * 11 % PEERS
            pltpu.make_async_remote_copy(
                src_ref=source.at[r],
                dst_ref=target.at[r],
                send_sem=a2a_send.at[chunk],
                recv_sem=a2a_recv.at[chunk],
                device_id=peer(r),
                device_id_type=MESH,
            ).start()

    def arrived(chunk):
        _, target = ends(chunk)
        rest = target.at[pl.ds(1, PEERS - 1)]
        pltpu.make_async_copy(rest, rest, a2a_recv.at[chunk]).wait()

    def sent(chunk):
        source, _ = ends(chunk)
        rest = source.at[pl.ds(1, PEERS - 1)]
        pltpu.make_async_copy(rest, rest, a2a_send.at[chunk]).wait()

    def placing(chunk):
        labels = recv0[:, :, FEAT:].reshape(PEERS * ROWS, TAIL).astype(F32)
        w = labels[:, 2 * chunk : 2 * chunk + 1]
        m = labels[:, 2 * chunk + 1 : 2 * chunk + 2]
        plane = lax.div(lax.rem(iota((PEERS * ROWS, 1), 0), ROWS), 2)
        key = m + (plane * 32).astype(F32)
        at = iota((PEERS * ROWS, 256), 1).astype(F32)
        spread = jnp.where(at == key, w, 0.0).T
        place[chunk] = spread.astype(BF16)
        total = jnp.sum(spread[:128], axis=1, keepdims=True)
        part0[4 * chunk : 4 * chunk + 4, :, FEAT:] = jnp.broadcast_to(total, (128, TAIL)).reshape(4, 32, TAIL)

    def accumulate(chunk):
        _, landed = ends(chunk)
        for t in range(FEAT // 256):
            block = landed[:, :, t * 256 : (t + 1) * 256].reshape(PEERS * ROWS, 256)
            numer = jnp.dot(place[chunk], block, preferred_element_type=F32).reshape(2, 4, 32, 256)
            part0[4 * chunk : 4 * chunk + 4, :, t * 256 : (t + 1) * 256] = numer[0]
            part1[4 * chunk : 4 * chunk + 4, :, t * 256 : (t + 1) * 256] = numer[1]

    parts, outs, rings = (part0, part1), (out0, out1), (ring0, ring1)

    def hop(h, way, k):
        return pltpu.make_async_remote_copy(
            src_ref=outs[h].at[way, k],
            dst_ref=rings[h].at[way, k],
            send_sem=ring_send.at[h, way, k],
            recv_sem=ring_recv.at[h, way, k],
            device_id=up if way == 0 else down,
            device_id_type=MESH,
        )

    def received(h, way, k):
        hop(h, way, k).wait_recv()
        if h == 0:
            tail = ring0[way, k, :, FEAT:].astype(jnp.int32).astype(F32)
            high, low = tail[:, 0:1], tail[:, 64:65]
            got[way, k] = jnp.broadcast_to((high * 1024.0 + low) * (1.0 / 512.0), (32, TAIL))
        unit = got[way, k][:, :1] * (LIMIT / LEVELS)
        return rings[h][way, k, :, :FEAT].astype(jnp.int32).astype(F32) * unit

    def step(k, way):
        index = 0 if k == 0 else (2 * k - 1 if way == 0 else 2 * k)
        for h in range(2):
            value = parts[h][index, :, :FEAT]
            joined = k > 1 or (k == 1 and way == 0)
            if joined:
                value = value + received(h, way, k - 1)
            if h == 0:
                weight = part0[index, :, FEAT:]
                if joined:
                    weight = weight + got[way, k - 1]
                units = weight * 512.0
                high = jnp.floor(units * (1.0 / 1024.0))
                low = units - high * 1024.0
                tail = jnp.where(iota((32, TAIL), 1) < 64, high, low)
                out0[way, k, :, FEAT:] = tail.astype(jnp.int32).astype(jnp.int16)
                per = (LEVELS / LIMIT) / jnp.maximum(weight, 0.25)[:, :1]
            level = jnp.floor(value * per + 0.5)
            outs[h][way, k, :, :FEAT] = level.astype(jnp.int32).astype(jnp.int16)
            hop(h, way, k).start()

    def finish(h):
        total = parts[h][15, :, :FEAT]
        for way in range(2):
            total = total + received(h, way, 7)
            if h == 0:
                part0[15, :, FEAT:] += got[way, 7]
        parts[h][15, :, :FEAT] = total

    pack(0)
    pl.semaphore_wait(barrier, PEERS + 1)
    send(0)
    pack(1)
    send(1)
    pack(2)
    send(2)
    pack(3)
    send(3)
    arrived(0)
    placing(0)
    accumulate(0)
    step(0, 0)
    step(1, 0)
    step(1, 1)
    placing(1)
    placing(2)
    placing(3)
    step(2, 0)
    arrived(1)
    accumulate(1)
    step(2, 1)
    step(3, 0)
    step(3, 1)
    step(4, 0)
    arrived(2)
    accumulate(2)
    step(4, 1)
    step(5, 0)
    step(5, 1)
    step(6, 0)
    arrived(3)
    accumulate(3)
    step(6, 1)
    step(7, 0)
    step(7, 1)
    finish(0)

    weight_sum = jnp.maximum(part0[15, :, FEAT:], 1.0)
    for r in range(8):
        t = part0[15, :, r * 128 : (r + 1) * 128] / weight_sum
        for b in range(4):
            tmpl[b, pl.ds(r, 8, stride=16), :] = t[8 * b : 8 * b + 8]
    finish(1)
    for r in range(8):
        t = part1[15, :, r * 128 : (r + 1) * 128] / weight_sum
        for b in range(4):
            tmpl[b, pl.ds(r + 8, 8, stride=16), :] = t[8 * b : 8 * b + 8]
    for b in range(4):
        window[0:BAND, 128 * b : 128 * (b + 1)] = tmpl[b].astype(BF16)

    below = pltpu.make_async_remote_copy(
        src_ref=window.at[pl.ds(BAND - ROWS, ROWS)], dst_ref=halo.at[0],
        send_sem=halo_send.at[0], recv_sem=halo_recv.at[0],
        device_id=(p, lax.rem(x + 1, NX)), device_id_type=MESH,
    )
    above = pltpu.make_async_remote_copy(
        src_ref=window.at[pl.ds(0, ROWS)], dst_ref=halo.at[1],
        send_sem=halo_send.at[1], recv_sem=halo_recv.at[1],
        device_id=(p, lax.rem(x + NX - 1, NX)), device_id_type=MESH,
    )
    below.start()
    above.start()

    stamp_rows = jnp.where(lax.div(iota((BAND, 8), 0), 16) == iota((BAND, 8), 1), 1.0, 0.0)
    stamp_cols = jnp.where(lax.div(iota((32, WIDTH), 1), 16) == iota((32, WIDTH), 0), 1.0, 0.0)
    good = jnp.where(good_ref[0] == 1, 1.0, 0.0)
    mask = jnp.dot(jnp.dot(stamp_rows, good, preferred_element_type=F32), stamp_cols, preferred_element_type=F32)
    design[:, 18] = mask.astype(BF16).reshape(8, ROWS, WIDTH)
    design[:, 19] = (science_ref[0].astype(F32) * mask).astype(BF16).reshape(8, ROWS, WIDTH)
    window[BAND + 2 * ROWS :, :] = jnp.zeros((256 - BAND - 2 * ROWS, WIDTH), BF16)
    load_vert.wait()
    load_horiz.wait()

    below.wait_recv()
    above.wait_recv()
    window[BAND : BAND + ROWS, :] = jnp.where(x > 0, halo[0].astype(F32), 0.0).astype(BF16)
    window[BAND + ROWS : BAND + 2 * ROWS, :] = jnp.where(x < NX - 1, halo[1].astype(F32), 0.0).astype(BF16)

    for f in range(3):
        rows = slice(f * 3 * BAND, (f + 1) * 3 * BAND)
        vimg[rows] = jnp.dot(vert[rows], window[...], preferred_element_type=F32).astype(BF16)

    for g in range(3):
        for i in range(3):
            count = (3 - i) * BAND
            image = jnp.dot(
                vimg[g * 3 * BAND : g * 3 * BAND + count], horiz[g * 3 + i], preferred_element_type=F32
            )
            for j in range(3 - i):
                k = g * 6 + BASIS_PAIRS.index((i, j))
                part = image[j * BAND : (j + 1) * BAND].astype(BF16).astype(F32) * mask
                design[:, k] = part.astype(BF16).reshape(8, ROWS, WIDTH)

    def product(q, sums):
        block = design[q].reshape(20 * ROWS, WIDTH)
        corner = block[16 * ROWS :]
        return tuple(
            total + lax.dot_general(a, b, (((1,), (1,)), ((), ())), preferred_element_type=F32)
            for total, a, b in zip(sums, (block, corner), (block[: 16 * ROWS], corner))
        )

    sums = lax.fori_loop(
        0, 8, product, (jnp.zeros((320, 256), F32), jnp.zeros((64, 64), F32)), unroll=True
    )

    def folded(total, first):
        high, wide = total.shape
        same = lax.rem(iota(total.shape, 0), ROWS) == lax.rem(iota(total.shape, 1), ROWS)
        total = jnp.sum(jnp.where(same, total, 0.0).reshape(high // ROWS, ROWS, wide), axis=1)
        fold = lax.div(iota((wide, 128), 0), ROWS) + first == iota((wide, 128), 1)
        fold = jnp.where(fold, 1.0, 0.0)
        return jnp.dot(total, fold, preferred_element_type=F32, precision=lax.Precision.HIGHEST)

    def blank(count):
        return jnp.zeros((count, 128), F32)

    left, right = folded(sums[0], 0), folded(sums[1], 16)
    mirror = jnp.concatenate([blank(16), left[16:20], blank(108)], axis=0).T[:24]
    normal = (
        jnp.concatenate([left, blank(4)], axis=0)
        + jnp.concatenate([blank(16), right, blank(4)], axis=0)
        + mirror
    )
    gram_mine[...] = normal
    gram_all[x] = normal

    shares = [
        pltpu.make_async_remote_copy(
            src_ref=gram_mine, dst_ref=gram_all.at[x],
            send_sem=gram_send.at[d - 1], recv_sem=gram_recv.at[d - 1],
            device_id=(p, lax.rem(x + d, NX)), device_id_type=MESH,
        )
        for d in range(1, NX)
    ]
    for share in shares:
        share.start()
    for share in shares:
        share.wait_recv()
    normal = gram_all[0] + gram_all[1] + gram_all[2] + gram_all[3]

    rows = iota((24, 128), 0)
    lanes = iota((24, 128), 1)
    diagonal = (rows == lanes) & (rows < 19)
    system = normal + jnp.where(diagonal, RIDGE * normal, 0.0)
    for k in range(19):
        pivot_row = system[k : k + 1] / system[k : k + 1, k : k + 1]
        column = jnp.where(rows[:, :1] == k, 0.0, system[:, k : k + 1])
        system = system - column * pivot_row
    rhs = system[:, 19:20]
    lead = jnp.sum(jnp.where(diagonal, system, 0.0), axis=1, keepdims=True)
    solved = rhs / jnp.where(rows[:, :1] < 19, lead, 1.0)
    coef_ref[...] = jnp.sum(jnp.where(diagonal, solved, 0.0), axis=0, keepdims=True)[:, :19]

    def model(q, carry):
        value = design[q, 19].astype(F32)
        for k in range(19):
            value = value - solved[k : k + 1] * design[q, k].astype(F32)
        diff_ref[0, pl.ds(q * ROWS, ROWS), :] = value.astype(BF16)
        return carry

    lax.fori_loop(0, 8, model, 0)

    for chunk in range(4):
        sent(chunk)
    for h in range(2):
        for way in range(2):
            for k in range(8):
                if k > 0 or way == 0:
                    hop(h, way, k).wait_send()
    below.wait_send()
    above.wait_send()
    for share in shares:
        share.wait_send()


def shards(pieces, piece_slot, piece_cell, weights, science, good_stamps):
    vmem = pl.BlockSpec(memory_space=pltpu.VMEM)
    anywhere = pl.BlockSpec(memory_space=pl.ANY)
    dma = pltpu.SemaphoreType.DMA
    return pl.pallas_call(
        kernel,
        out_shape=(
            jax.ShapeDtypeStruct((1, BAND, WIDTH), BF16),
            jax.ShapeDtypeStruct((1, 19), F32),
        ),
        in_specs=[vmem] * 5 + [anywhere] * 3,
        out_specs=(vmem, vmem),
        scratch_shapes=[
            pltpu.VMEM((512, 2048), BF16),
            pltpu.VMEM((9 * BAND, 256), BF16),
            pltpu.VMEM((9, WIDTH, WIDTH), BF16),
            pltpu.VMEM((4, 2, 128, 512), BF16),
            pltpu.VMEM((PEERS, ROWS, FEAT + TAIL), BF16),
            pltpu.VMEM((3, PEERS, ROWS, FEAT), BF16),
            pltpu.VMEM((PEERS, ROWS, FEAT + TAIL), BF16),
            pltpu.VMEM((3, PEERS, ROWS, FEAT), BF16),
            pltpu.VMEM((4, 256, PEERS * ROWS), BF16),
            pltpu.VMEM((NZ, 32, FEAT + TAIL), F32),
            pltpu.VMEM((NZ, 32, FEAT), F32),
            pltpu.VMEM((2, 8, 32, FEAT + TAIL), jnp.int16),
            pltpu.VMEM((2, 8, 32, FEAT), jnp.int16),
            pltpu.VMEM((2, 8, 32, FEAT + TAIL), jnp.int16),
            pltpu.VMEM((2, 8, 32, FEAT), jnp.int16),
            pltpu.VMEM((2, 8, 32, TAIL), F32),
            pltpu.VMEM((4, BAND, 128), F32),
            pltpu.VMEM((256, WIDTH), BF16),
            pltpu.VMEM((2, ROWS, WIDTH), BF16),
            pltpu.VMEM((9 * BAND, WIDTH), BF16),
            pltpu.VMEM((8, 20, ROWS, WIDTH), BF16),
            pltpu.VMEM((24, 128), F32),
            pltpu.VMEM((NX, 24, 128), F32),
            dma((3,)),
            dma((4,)),
            dma((4,)),
            dma((2, 2, 8)),
            dma((2, 2, 8)),
            dma((2,)),
            dma((2,)),
            dma((3,)),
            dma((3,)),
        ],
        compiler_params=pltpu.CompilerParams(
            collective_id=0, has_side_effects=True, vmem_limit_bytes=56 * 2**20
        ),
    )(
        piece_slot[0], piece_cell[0], weights[0], science, good_stamps, pieces,
        jnp.asarray(vertical_matrix()), jnp.asarray(horizontal_matrix()),
    )


def solution(mesh):
    in_specs = (
        P("patch", "sub", None, None),
        P("patch", "sub", None),
        P("patch", "sub", None),
        P("patch", "sub", None),
        P("patch", "sub", None),
        P("patch", "sub", None),
    )
    out_specs = (P("patch", "sub", None), P("patch", None))
    return jax.shard_map(shards, mesh=mesh, in_specs=in_specs, out_specs=out_specs, check_vma=False)
```
